32 devices in a mesh: dp: 8 (over z, x), shard: 4 (over y, core).
Axes of the slice: x: 2, y: 2, z: 4, core: 2. Of those that a mesh axis runs over, the one named last changes fastest.
Arguments:
- tokens: bfloat16 [32768, 640], P(('dp', 'shard')), may hold values from -6 to 6
- out_grad: bfloat16 [32768, 640], P(('dp', 'shard')), may hold values from -6 to 6
- query_weight: float32 [640, 1024], P(None, 'shard'), may hold values from -0.25 to 0.25
- query_first: float32 [640, 1024], P(None, 'shard'), may hold values from -128 to 128
- query_second: float32 [640, 1024], P(None, 'shard'), may hold values from 1724 to 6898
- key_value_weight: float32 [2, 640, 256], P(None, 'shard'), may hold values from -0.25 to 0.25
- key_value_first: float32 [2, 640, 256], P(None, 'shard'), may hold values from -128 to 128
- key_value_second: float32 [2, 640, 256], P(None, 'shard'), may hold values from 1724 to 6898
- output_weight: float32 [1024, 640], P('shard'), may hold values from -3 to 3
- output_first: float32 [1024, 640], P('shard'), may hold values from -6 to 6
- output_second: float32 [1024, 640], P('shard'), may hold values from 6.736842 to 26.947369
- gate_up_weight: float32 [2, 640, 2048], P(None, None, 'shard'), may hold values from -0.25 to 0.25
- gate_up_first: float32 [2, 640, 2048], P(None, None, 'shard'), may hold values from -128 to 128
- gate_up_second: float32 [2, 640, 2048], P(None, None, 'shard'), may hold values from 1724 to 6898
- down_weight: float32 [2048, 640], P('shard'), may hold values from -0.125 to 0.125
- down_first: float32 [2048, 640], P('shard'), may hold values from -128 to 128
- down_second: float32 [2048, 640], P('shard'), may hold values from 1724 to 6898
- gain_values: float32 [2, 640], P(None, 'shard'), may hold values from 0.5 to 1.5
- gain_first: float32 [2, 640], P(None, 'shard'), may hold values from -256 to 256
- gain_second: float32 [2, 640], P(None, 'shard'), may hold values from 6898 to 27594
Outputs:
- block_output: bfloat16 [32768, 640], P(('dp', 'shard'))
- tokens_grad: float32 [32768, 640], P(('dp', 'shard'))
- query_new: float32 [640, 1024], P(None, 'shard')
- query_first_new: float32 [640, 1024], P(None, 'shard')
- query_second_new: float32 [640, 1024], P(None, 'shard')
- key_value_new: float32 [2, 640, 256], P(None, 'shard')
- key_value_first_new: float32 [2, 640, 256], P(None, 'shard')
- key_value_second_new: float32 [2, 640, 256], P(None, 'shard')
- output_new: float32 [1024, 640], P('shard')
- output_first_new: float32 [1024, 640], P('shard')
- output_second_new: float32 [1024, 640], P('shard')
- gate_up_new: float32 [2, 640, 2048], P(None, None, 'shard')
- gate_up_first_new: float32 [2, 640, 2048], P(None, None, 'shard')
- gate_up_second_new: float32 [2, 640, 2048], P(None, None, 'shard')
- down_new: float32 [2048, 640], P('shard')
- down_first_new: float32 [2048, 640], P('shard')
- down_second_new: float32 [2048, 640], P('shard')
- gain_new: float32 [2, 640], P(None, 'shard')
- gain_first_new: float32 [2, 640], P(None, 'shard')
- gain_second_new: float32 [2, 640], P(None, 'shard')
The draws below stay inside these ranges and needn't reach their ends.
All inputs are finite; a program needn't handle non-finite values.
Results may differ from the reference program's by a relative error of at most 0.025.
Values may be sent and summed in bfloat16 or wider, within the bound.
No kernel may reach another device: no remote copies, remote signals or barrier semaphores. Data moves between devices by JAX's collectives and lax.ppermute only.
A program may use at most 256 MiB of HBM per device.

```python
import math
import jax
import jax.numpy as jnp
from jax import lax

D = 640
HEADS = 4
HD = 256
FF = 2048
WINDOW = 512
STEP = 10
SEQ = 4096
TOKENS = 32768


def steps_of(key, extent, cuts, low, largest):
    level = 1.0
    for dim, blocks in cuts:
        steps = jax.random.uniform(jax.random.fold_in(jax.random.fold_in(key, 6), dim), (blocks,), jnp.float32, low / len(cuts), largest / len(cuts))
        level = level * jnp.repeat(jnp.exp(steps), extent[dim] // blocks).reshape((-1,) + (1,) * (len(extent) - 1 - dim))
    return level


def gaussian(key, extent, spread, limit, shards=(), kind=jnp.bfloat16):
    values = jax.random.normal(key, extent, jnp.float32) * spread
    if len(shards) > 0:
        values = steps_of(key, extent, shards, -0.22, 0.18) * values
    return jnp.clip(values, min=-limit, max=limit).astype(kind)


def setup_inputs(seed: int = 0) -> dict:
    seeds = jax.random.split(jax.random.key(seed), 21)
    return {
        "tokens": gaussian(seeds[0], (TOKENS, D), 1.0, 6.0, ((0, 32),)),
        "out_grad": gaussian(seeds[1], (TOKENS, D), 1.0, 6.0, ((0, 32),)),
        "query_weight": gaussian(seeds[2], (D, HEADS * HD), D ** -0.5, 0.25, ((1, 4),), jnp.float32),
        "query_first": gaussian(seeds[3], (D, HEADS * HD), ((TOKENS // 81) ** 0.5), 128.0, ((1, 4),), jnp.float32),
        "query_second": jnp.clip(jnp.exp(math.log(6898.0) - 1.3865843422731479 * jax.random.uniform(seeds[4], (D, HEADS * HD), jnp.float32) ** steps_of(seeds[4], (D, HEADS * HD), ((1, 4),), -0.2, 0.2)), 1724.0, 6898.0),
        "key_value_weight": gaussian(seeds[5], (2, D, HD), D ** -0.5, 0.25, ((1, 4),), jnp.float32),
        "key_value_first": gaussian(seeds[6], (2, D, HD), ((TOKENS // 81) ** 0.5), 128.0, ((1, 4),), jnp.float32),
        "key_value_second": jnp.clip(jnp.exp(math.log(6898.0) - 1.3865843422731479 * jax.random.uniform(seeds[7], (2, D, HD), jnp.float32) ** steps_of(seeds[7], (2, D, HD), ((1, 4),), -0.2, 0.2)), 1724.0, 6898.0),
        "output_weight": gaussian(seeds[8], (HEADS * HD, D), (HEADS * HD // (WINDOW // 2)) ** -0.5, 3.0, ((0, 4),), jnp.float32),
        "output_first": gaussian(seeds[9], (HEADS * HD, D), ((2 * TOKENS) ** 0.5 * (81 * WINDOW) ** -0.5), 6.0, ((0, 4),), jnp.float32),
        "output_second": jnp.clip(jnp.exp(math.log(26.947369) - 1.3862944 * jax.random.uniform(seeds[10], (HEADS * HD, D), jnp.float32) ** steps_of(seeds[10], (HEADS * HD, D), ((0, 4),), -0.2, 0.2)), 6.736842, 26.947369),
        "gate_up_weight": gaussian(seeds[11], (2, D, FF), D ** -0.5, 0.25, ((2, 4),), jnp.float32),
        "gate_up_first": gaussian(seeds[12], (2, D, FF), ((TOKENS // 81) ** 0.5), 128.0, ((2, 4),), jnp.float32),
        "gate_up_second": jnp.clip(jnp.exp(math.log(6898.0) - 1.3865843422731479 * jax.random.uniform(seeds[13], (2, D, FF), jnp.float32) ** steps_of(seeds[13], (2, D, FF), ((2, 4),), -0.2, 0.2)), 1724.0, 6898.0),
        "down_weight": gaussian(seeds[14], (FF, D), FF ** -0.5, 0.125, ((0, 4),), jnp.float32),
        "down_first": gaussian(seeds[15], (FF, D), ((TOKENS // 81) ** 0.5), 128.0, ((0, 4),), jnp.float32),
        "down_second": jnp.clip(jnp.exp(math.log(6898.0) - 1.3865843422731479 * jax.random.uniform(seeds[16], (FF, D), jnp.float32) ** steps_of(seeds[16], (FF, D), ((0, 4),), -0.2, 0.2)), 1724.0, 6898.0),
        "gain_values": jnp.clip(1.0 + 0.1 * jax.random.normal(seeds[17], (2, D), jnp.float32), 0.5, 1.5),
        "gain_first": gaussian(seeds[18], (2, D), ((4 * TOKENS // 81) ** 0.5), 256.0, ((1, 4),), jnp.float32),
        "gain_second": jnp.clip(jnp.exp(math.log(27594.0) - 1.3863668 * jax.random.uniform(seeds[19], (2, D), jnp.float32) ** steps_of(seeds[19], (2, D), ((1, 4),), -0.2, 0.2)), 6898.0, 27594.0),
    }


EPSILON = 1e-06
BETA_ONE = 0.9
BETA_TWO = 0.95
ADAM_EPSILON = 1e-08
WEIGHT_DECAY = 0.1
NEGATIVE = -1e+30
GAIN_RATE = 0.6

@jax.custom_vjp
def low(v):
    return lax.optimization_barrier(v.astype(jnp.bfloat16)).astype(jnp.float32)

@jax.custom_vjp
def low_back(v):
    return v

def low_keep(v):
    return (low(v), None)

def low_pass(kept, grad):
    return (grad,)

def back_keep(v):
    return (v, None)

def back_low(kept, grad):
    return (low(grad),)
low.defvjp(low_keep, low_pass)
low_back.defvjp(back_keep, back_low)

def low_both(value):
    return low_back(low(value))

def exact_dot(left, right):
    return jnp.dot(left, right, precision=lax.Precision.HIGHEST, preferred_element_type=jnp.float32)

def rms_scale(values, gain):
    return values * lax.rsqrt(lax.optimization_barrier(jnp.mean(values * values, axis=-1, keepdims=True)) + EPSILON) * gain

def attend(pieces):
    queries, key_slab, value_slab = pieces
    length = queries.shape[0]
    scores = jnp.einsum('shd,td->hst', queries, key_slab, precision=lax.Precision.HIGHEST) * HD ** (-0.5)
    scores = low_back(scores)
    places = jnp.arange(length, dtype=jnp.int32)
    offset = places[:, None] - places[None, :]
    allowed = (offset >= 0) & (offset < WINDOW)
    scores = jnp.where(allowed[None], scores, NEGATIVE)
    row_top = lax.optimization_barrier(jnp.max(scores, axis=-1, keepdims=True))
    weights = jnp.exp(scores - row_top)
    probs = low(weights / lax.optimization_barrier(jnp.sum(weights, axis=-1, keepdims=True)))
    return jnp.einsum('hst,td->shd', probs, value_slab, precision=lax.Precision.HIGHEST)

def forward(inputs, query_w, key_value_w, output_w, gate_up_w, down_w, gain_w):
    normed = low(rms_scale(inputs, gain_w[0]))
    queries = low_both(exact_dot(normed, query_w))
    key_all = low_both(exact_dot(normed, key_value_w[0]))
    value_all = low_both(exact_dot(normed, key_value_w[1]))
    seq_count = inputs.shape[0] // SEQ
    mixed = lax.map(jax.checkpoint(attend), (queries.reshape(seq_count, SEQ, HEADS, HD), key_all.reshape(seq_count, SEQ, HD), value_all.reshape(seq_count, SEQ, HD)))
    mixed = low_both(mixed.reshape(inputs.shape[0], HEADS * HD))
    middle = inputs + low_back(exact_dot(mixed, output_w))
    second_norm = low(rms_scale(middle, gain_w[1]))
    gate_proj = low_back(exact_dot(second_norm, gate_up_w[0]))
    up_proj = low_back(exact_dot(second_norm, gate_up_w[1]))
    activated = low(jax.nn.gelu(gate_proj, approximate=True) * up_proj)
    return middle + low_back(exact_dot(activated, down_w))

def rate_list():
    return (2.0 / D ** 0.5, 2.0 / D ** 0.5, 2.0 / (HEADS * HD // (WINDOW // 2)) ** 0.5, 2.0 / D ** 0.5, 2.0 / FF ** 0.5, GAIN_RATE)

def adam_step(weight, first, second, grad, rate):
    first_new = BETA_ONE * first + (1.0 - BETA_ONE) * grad
    second_new = BETA_TWO * second + (1.0 - BETA_TWO) * grad * grad
    first_hat = first_new / (1.0 - BETA_ONE ** STEP)
    second_hat = second_new / (1.0 - BETA_TWO ** STEP)
    updated = weight - rate * (first_hat / (jnp.sqrt(second_hat) + ADAM_EPSILON) + WEIGHT_DECAY * weight)
    return (updated, first_new, second_new)

def reference(tokens, out_grad, query_weight, query_first, query_second, key_value_weight, key_value_first, key_value_second, output_weight, output_first, output_second, gate_up_weight, gate_up_first, gate_up_second, down_weight, down_first, down_second, gain_values, gain_first, gain_second):
    masters = (query_weight, key_value_weight, output_weight, gate_up_weight, down_weight, gain_values)
    firsts = (query_first, key_value_first, output_first, gate_up_first, down_first, gain_first)
    seconds = (query_second, key_value_second, output_second, gate_up_second, down_second, gain_second)
    rounded = tuple((low(weight) for weight in masters))
    result, pullback = jax.vjp(forward, tokens.astype(jnp.float32), *rounded)
    grads = pullback(out_grad.astype(jnp.float32))
    rates = rate_list()
    updates = [adam_step(masters[index], firsts[index], seconds[index], grads[index + 1], rates[index]) for index in range(6)]
    return (result.astype(jnp.bfloat16), grads[0], updates[0][0], updates[0][1], updates[0][2], updates[1][0], updates[1][1], updates[1][2], updates[2][0], updates[2][1], updates[2][2], updates[3][0], updates[3][1], updates[3][2], updates[4][0], updates[4][1], updates[4][2], updates[5][0], updates[5][1], updates[5][2])
```

```python
import functools

import jax
import jax.numpy as jnp
from jax import lax
from jax.experimental import pallas as pl
from jax.experimental.pallas import tpu as pltpu
from jax.sharding import PartitionSpec as P

D = 640
HEADS = 4
HD = 256
FF = 2048
WINDOW = 512
STEP = 10

EPSILON = 1e-06
BETA_ONE = 0.9
BETA_TWO = 0.95
ADAM_EPSILON = 1e-08
WEIGHT_DECAY = 0.1
NEGATIVE = -1e30
GAIN_RATE = 0.6

BLOCK = 256
SPAN = WINDOW + BLOCK
PAIR = 2 * HD
PART = FF // 4
KV_ROWS = D // 4
LOG2E = 1.4426950408889634
SCORE_SCALE = HD**-0.5
GELU_A = 0.7978845608028654
GELU_B = GELU_A * 0.044715

BF16 = jnp.bfloat16
F32 = jnp.float32
ANYWHERE = pl.BlockSpec(memory_space=pl.ANY)
IN_HBM = pl.BlockSpec(memory_space=pltpu.HBM)
IN_VMEM = pl.BlockSpec(memory_space=pltpu.VMEM)
IN_SMEM = pl.BlockSpec(memory_space=pltpu.SMEM)


def dot(left, right):
    return lax.dot_general(left, right, (((1,), (0,)), ((), ())), preferred_element_type=F32)


def dot_nt(left, right):
    return lax.dot_general(left, right, (((1,), (1,)), ((), ())), preferred_element_type=F32)


LONG, SHORT = 40 << 30, 1 << 20


def call(kernel, cost, vmem, **kwargs):
    return pl.pallas_call(
        kernel,
        compiler_params=pltpu.CompilerParams(vmem_limit_bytes=vmem << 20),
        cost_estimate=pl.CostEstimate(flops=cost, bytes_accessed=0, transcendentals=0),
        **kwargs,
    )


def shape(dims, kind):
    return jax.ShapeDtypeStruct(dims, kind)


def in_hbm(dims, kind):
    return pltpu.HBM(dims, kind)


def stay(values):
    return [pltpu.with_memory_space_constraint(v, pltpu.HBM) for v in values]


def row_mean(values):
    return jnp.mean(values, axis=-1, keepdims=True)


def blocks(rows, size=BLOCK):
    return [slice(start, start + size) for start in range(0, rows, size)]


class Copies:
    def __init__(self, sems):
        self.sems = sems
        self.count = 0
        self.stores = []

    def load(self, source, target):
        copy = pltpu.make_async_copy(source, target, self.sems.at[self.count])
        self.count += 1
        copy.start()
        return copy

    def store(self, source, target):
        self.stores.append(self.load(source, target))

    def finish(self):
        for copy in self.stores:
            copy.wait()


def key_value_kernel(old_ref, own_ref, gain_ref, w_ref, h_ref, ht_ref, kv_ref):
    x = jnp.where(pl.program_id(0) < 2, old_ref[...], own_ref[...]).astype(F32)
    h = x * lax.rsqrt(row_mean(x * x) + EPSILON) * gain_ref[0:1, :]
    ht_ref[...] = h.T.astype(BF16)
    h = h.astype(BF16)
    h_ref[...] = h
    kv_ref[0] = dot(h, w_ref[0]).astype(BF16)
    kv_ref[1] = dot(h, w_ref[1]).astype(BF16)


def key_value(halo, tokens, gains, weights):
    rows = tokens.shape[0]
    slab = rows + WINDOW
    own = lambda i: jnp.maximum(i - 2, 0)
    return call(
        key_value_kernel,
        SHORT,
        12,
        grid=(slab // BLOCK,),
        in_specs=[
            pl.BlockSpec((BLOCK, D), lambda i: (jnp.minimum(i, 1), 0)),
            pl.BlockSpec((BLOCK, D), lambda i: (own(i), 0)),
            pl.BlockSpec((2, D), lambda i: (0, 0)),
            pl.BlockSpec((2, D, HD), lambda i: (0, 0, 0)),
        ],
        out_specs=[
            pl.BlockSpec((BLOCK, D), lambda i: (own(i), 0)),
            pl.BlockSpec((D, BLOCK), lambda i: (0, i)),
            pl.BlockSpec((2, BLOCK, HD), lambda i: (0, i, 0)),
        ],
        out_shape=[shape((rows, D), BF16), in_hbm((D, slab), BF16), shape((2, slab, HD), BF16)],
    )(halo, tokens, gains, weights)


def triangle():
    key = lax.broadcasted_iota(jnp.int32, (BLOCK, BLOCK), 0)
    query = lax.broadcasted_iota(jnp.int32, (BLOCK, BLOCK), 1)
    return key <= query


def join(own, scores, bias_old, bias_mid):
    oldest, middle = scores[:BLOCK], scores[BLOCK : 2 * BLOCK]
    if bias_old is not None:
        oldest = oldest + bias_old
    if bias_mid is not None:
        middle = middle + bias_mid
    return jnp.where(own, scores[2 * BLOCK :], oldest), middle


def biases(bias_ref, block):
    return (bias_ref[0] if block < 2 else None, bias_ref[0] if block < 1 else None)


def attend_kernel(last, bias_ref, gain_ref, h_hbm, kv_hbm, wa_hbm, wb_hbm, x_hbm, *rest):
    if last:
        q_hbm, a_hbm, lse_ref, y_hbm, h2_hbm, h2t_hbm = rest[:6]
        h, kv, w, x, q, a, y, values_t, h2, h2t, sems = rest[6:]
    else:
        q_hbm, a_hbm, lse_ref, y_hbm = rest[:4]
        h, kv, w, x, q, a, y, values_t, sems = rest[4:]
    rows_all = h.shape[0]
    copies = Copies(sems)
    first = [copies.load(h_hbm, h), copies.load(wa_hbm, w.at[0]), copies.load(wb_hbm, w.at[1])]
    second = copies.load(kv_hbm, kv)
    third = copies.load(x_hbm, x)
    for copy in first:
        copy.wait()
    for head in range(2):
        q[:, head * HD : (head + 1) * HD] = dot(h[...], w[head, 0]).astype(BF16)
    copies.store(q, q_hbm)
    second.wait()
    values_t[...] = kv[1].T
    third.wait()
    own = triangle()
    scale = SCORE_SCALE * LOG2E
    zero = jnp.zeros((BLOCK, BLOCK), F32)
    for block, rows in enumerate(blocks(rows_all)):
        span = slice(block * BLOCK, block * BLOCK + SPAN)
        for head in range(2):
            cols = slice(head * HD, (head + 1) * HD)
            scores = dot_nt(kv[0, span], q[rows, cols])
            joined, middle = join(own, scores, *biases(bias_ref, block))
            top = jnp.max(jnp.maximum(joined, middle), axis=0, keepdims=True)
            p_joined = jnp.exp2((joined - top) * scale)
            p_middle = jnp.exp2((middle - top) * scale)
            total = jnp.sum(p_joined + p_middle, axis=0, keepdims=True)
            probs = jnp.concatenate(
                [
                    jnp.where(own, zero, p_joined).astype(BF16),
                    p_middle.astype(BF16),
                    jnp.where(own, p_joined, zero).astype(BF16),
                ],
                axis=0,
            )
            mixed = dot(values_t[:, span], probs) * (1.0 / total)
            a[rows, cols] = mixed.T.astype(BF16)
            lse_ref[head : head + 1, rows] = top * scale + jnp.log2(total)
        copies.store(a.at[rows], a_hbm.at[rows])
    for rows in blocks(rows_all):
        total_y = x[rows].astype(F32)
        total_y = total_y + dot_nt(a[rows, :HD], w[0, 1]) + dot_nt(a[rows, HD:], w[1, 1])
        y[rows] = total_y
        copies.store(y.at[rows], y_hbm.at[rows])
        if last:
            normal = total_y * lax.rsqrt(row_mean(total_y * total_y) + EPSILON)
            normal = normal * gain_ref[1:2, :]
            h2[rows] = normal.astype(BF16)
            h2t[:, rows] = normal.T.astype(BF16)
            copies.store(h2.at[rows], h2_hbm.at[rows])
            copies.store(h2t.at[:, rows], h2t_hbm.at[:, rows])
    copies.finish()


def attend(bias, gains, normed, kv, weights, base, last):
    rows = normed.shape[0]
    slab = rows + WINDOW
    more = [shape((rows, D), BF16), shape((D, rows), BF16)] if last else []
    return call(
        functools.partial(attend_kernel, last),
        SHORT if last else LONG,
        20,
        in_specs=[IN_SMEM, IN_VMEM] + [ANYWHERE] * 4 + [IN_HBM],
        out_specs=[IN_HBM, IN_HBM, IN_VMEM, IN_HBM] + [ANYWHERE] * len(more),
        out_shape=[
            in_hbm((rows, PAIR), BF16),
            in_hbm((rows, PAIR), BF16),
            shape((8, rows), F32),
            in_hbm((rows, D), F32),
        ]
        + more,
        scratch_shapes=[
            pltpu.VMEM((rows, D), BF16),
            pltpu.VMEM((2, slab, HD), BF16),
            pltpu.VMEM((2, 2, D, HD), BF16),
            pltpu.VMEM((rows, D), base.dtype),
            pltpu.VMEM((rows, PAIR), BF16),
            pltpu.VMEM((rows, PAIR), BF16),
            pltpu.VMEM((rows, D), F32),
            pltpu.VMEM((HD, slab), BF16),
        ]
        + [pltpu.VMEM(m.shape, m.dtype) for m in more]
        + [pltpu.SemaphoreType.DMA((24,))],
    )(bias, gains, normed, kv, *weights, *(stay([base]) if last else [base]))


def attend_back_kernel(
    part, bias_ref, gain_ref, lsa_ref, lsb_ref,
    d_hbm, y_hbm, c_hbm, kv_hbm, qa_hbm, qb_hbm, aa_hbm, ab_hbm, ht_hbm, wkv_hbm,
    w0_hbm, w1_hbm, w2_hbm, w3_hbm, *rest,
):
    if part:
        g_in, gkv_in, gain_in = rest[:3]
        dy_hbm, dq_hbm, dk_hbm, dv_hbm, even_out, odd_out, gkv_out, gain_out = rest[3:11]
        rest = rest[11:]
    else:
        dy_hbm, dq_hbm, dk_hbm, dv_hbm, g_out, gkv_out, gain_out, halo_out = rest[:8]
        rest = rest[8:]
    (
        d, y, c, kv, q, a, ht, w, wkv, dy, do, do_t, da, dq, dk, dv, dkv, p_all, ds_all, g, gkv, sems,
    ) = rest
    row0 = part * WINDOW
    mine = pl.ds(row0, WINDOW)
    copies = Copies(sems)
    weights = (w0_hbm, w1_hbm, w2_hbm, w3_hbm)
    first = [copies.load(y_hbm.at[mine], y), copies.load(c_hbm.at[mine], c)]
    first.append(copies.load(d_hbm.at[mine], d))
    second = [copies.load(p, w.at[i]) for i, p in enumerate(weights)]
    second.append(copies.load(kv_hbm.at[:, pl.ds(row0, 2 * WINDOW)], kv))
    second.append(copies.load(qa_hbm.at[mine], q.at[0]))
    second.append(copies.load(qb_hbm.at[mine], q.at[1]))
    third = [
        copies.load(aa_hbm.at[mine], a.at[0]),
        copies.load(ab_hbm.at[mine], a.at[1]),
        copies.load(ht_hbm.at[:, pl.ds(row0, 2 * WINDOW)], ht),
    ]
    if part:
        third += [copies.load(g_in, g), copies.load(gkv_in, gkv), copies.load(wkv_hbm, wkv)]

    for copy in first:
        copy.wait()
    gain = gain_ref[1:2, :]
    d_gain = gain_in[...] if part else jnp.zeros((1, D), F32)
    for rows in blocks(WINDOW):
        values = y[rows]
        dh = d[rows]
        r = lax.rsqrt(row_mean(values * values) + EPSILON)
        n = values * r
        inner = dh * gain
        grad = c[rows].astype(F32) + r * (inner - n * row_mean(inner * n))
        d_gain = d_gain + jnp.sum(dh * n, axis=0, keepdims=True)
        dy[rows] = grad
        do[rows] = grad.astype(BF16)
        do_t[:, rows] = grad.T.astype(BF16)
    copies.store(dy, dy_hbm)
    for copy in second:
        copy.wait()
    for head in range(HEADS):
        da[head] = dot(do[...], w[head, 1]).astype(BF16)

    own = triangle()
    scale = SCORE_SCALE * LOG2E
    zero = jnp.zeros((BLOCK, BLOCK), F32)
    for block, rows in enumerate(blocks(WINDOW)):
        span = slice(block * BLOCK, block * BLOCK + SPAN)
        keys, values = kv[0, span], kv[1, span]
        keys_t = keys.T
        for head in range(HEADS):
            cols = slice(head * HD, (head + 1) * HD)
            side, pair = head // 2, slice(head % 2 * HD, head % 2 * HD + HD)
            scores = dot_nt(keys, q[side, rows, pair])
            back = dot_nt(values, da[head, rows])
            lse_ref = (lsa_ref, lsb_ref)[side]
            lse = lse_ref[head % 2 : head % 2 + 1, row0 + block * BLOCK : row0 + block * BLOCK + BLOCK]
            joined, middle = join(own, scores, *biases(bias_ref, 2 * part + block))
            p_joined = jnp.exp2(joined * scale - lse)
            p_middle = jnp.exp2(middle * scale - lse)
            b_joined, b_middle = join(own, back, None, None)
            delta = jnp.sum(p_joined * b_joined + p_middle * b_middle, axis=0, keepdims=True)
            s_joined = p_joined * (b_joined - delta)
            s_middle = p_middle * (b_middle - delta)
            p_all[block, :BLOCK, cols] = jnp.where(own, zero, p_joined).astype(BF16)
            p_all[block, BLOCK : 2 * BLOCK, cols] = p_middle.astype(BF16)
            p_all[block, 2 * BLOCK :, cols] = jnp.where(own, p_joined, zero).astype(BF16)
            ds_all[block, :BLOCK, cols] = jnp.where(own, zero, s_joined).astype(BF16)
            ds_all[block, BLOCK : 2 * BLOCK, cols] = s_middle.astype(BF16)
            ds_all[block, 2 * BLOCK :, cols] = jnp.where(own, s_joined, zero).astype(BF16)
            grad = dot(keys_t, ds_all[block, :, cols]) * SCORE_SCALE
            dq[rows, cols] = grad.T.astype(BF16)
        da_rows = jnp.concatenate([da[h, rows] for h in range(HEADS)], axis=0)
        q_rows = jnp.concatenate(
            [q[h // 2, rows, h % 2 * HD : h % 2 * HD + HD] for h in range(HEADS)], axis=0
        )
        block_dv = dot(p_all[block], da_rows)
        block_dk = dot(ds_all[block], q_rows) * SCORE_SCALE
        if block == 0:
            dv[:SPAN] = block_dv
            dk[:SPAN] = block_dk
        else:
            dv[BLOCK:SPAN] += block_dv[:WINDOW]
            dk[BLOCK:SPAN] += block_dk[:WINDOW]
            dv[SPAN:] = block_dv[WINDOW:]
            dk[SPAN:] = block_dk[WINDOW:]
    copies.store(dq, dq_hbm)
    if part:
        copies.store(dk, dk_hbm)
        copies.store(dv, dv_hbm)
    else:
        copies.store(dk.at[pl.ds(WINDOW, WINDOW)], dk_hbm)
        copies.store(dv.at[pl.ds(WINDOW, WINDOW)], dv_hbm)
        halo_out[0] = dk[:WINDOW].astype(BF16)
        halo_out[1] = dv[:WINDOW].astype(BF16)
    for copy in third:
        copy.wait()
    first_gain = jnp.zeros((D, HD), F32)
    for slot, head in enumerate((0, 2, 1, 3)):
        pair = slice(head % 2 * HD, head % 2 * HD + HD)
        d_wq = dot(ht[:, WINDOW:], dq[:, head * HD : (head + 1) * HD])
        d_wo = dot(do_t[...], a[head // 2, :, pair])
        if part:
            d_wq = d_wq + g[slot, 0].astype(F32)
            d_wo = d_wo + g[slot, 1].astype(F32)
            first_gain = first_gain + d_wq * w[head, 0].astype(F32)
        g[slot, 0] = d_wq.astype(BF16)
        g[slot, 1] = d_wo.astype(BF16)
        if part and slot == 1:
            copies.store(g.at[pl.ds(0, 2)], even_out)
    copies.store(*((g.at[pl.ds(2, 2)], odd_out) if part else (g, g_out)))
    for i, grad in enumerate((dk, dv)):
        dkv[...] = grad[...].astype(BF16)
        d_w = dot(ht[...], dkv[...])
        if part:
            d_w = d_w + gkv[i].astype(F32)
            first_gain = first_gain + d_w * wkv[i].astype(F32)
        gkv[i] = d_w.astype(BF16)
    copies.store(gkv, gkv_out)
    if part:
        lanes = first_gain[:, :128] + first_gain[:, 128:]
        gain_out[0:1, :] = jnp.sum(lanes.T, axis=0, keepdims=True) / gain_ref[0:1, :]
        gain_out[1:2, :] = d_gain
    else:
        gain_out[...] = d_gain
    copies.finish()


def attend_back(part, bias, gains, lses, arrays, weights, sums):
    width = HEADS * HD
    slab = 2 * WINDOW
    many, pair_of = (4, 2, D, HD), (2, 2, D, HD)
    own_rows = slab if part else WINDOW
    outs = [
        in_hbm((WINDOW, D), F32),
        in_hbm((WINDOW, width), BF16),
        in_hbm((own_rows, HD), F32),
        in_hbm((own_rows, HD), F32),
    ]
    if part:
        outs += [shape(pair_of, BF16), shape(pair_of, BF16), shape((2, D, HD), BF16)]
        outs += [shape((2, D), F32)]
        out_specs = [ANYWHERE] * 7 + [IN_VMEM]
    else:
        outs += [in_hbm(many, BF16), in_hbm((2, D, HD), BF16), shape((1, D), F32)]
        outs += [shape((2, WINDOW, HD), BF16)]
        out_specs = [ANYWHERE] * 6 + [IN_VMEM] * 2
    return call(
        functools.partial(attend_back_kernel, part),
        LONG,
        42,
        in_specs=[IN_SMEM, IN_VMEM, IN_VMEM, IN_VMEM]
        + [ANYWHERE] * 14
        + ([ANYWHERE] * 2 + [IN_VMEM] if part else []),
        out_specs=out_specs,
        out_shape=outs,
        scratch_shapes=[
            pltpu.VMEM((WINDOW, D), F32),
            pltpu.VMEM((WINDOW, D), F32),
            pltpu.VMEM((WINDOW, D), BF16),
            pltpu.VMEM((2, slab, HD), BF16),
            pltpu.VMEM((2, WINDOW, PAIR), BF16),
            pltpu.VMEM((2, WINDOW, PAIR), BF16),
            pltpu.VMEM((D, slab), BF16),
            pltpu.VMEM((HEADS, 2, D, HD), BF16),
            pltpu.VMEM((2, D, HD), BF16),
            pltpu.VMEM((WINDOW, D), F32),
            pltpu.VMEM((WINDOW, D), BF16),
            pltpu.VMEM((D, WINDOW), BF16),
            pltpu.VMEM((HEADS, WINDOW, HD), BF16),
            pltpu.VMEM((WINDOW, width), BF16),
            pltpu.VMEM((slab, HD), F32),
            pltpu.VMEM((slab, HD), F32),
            pltpu.VMEM((slab, HD), BF16),
            pltpu.VMEM((2, SPAN, width), BF16),
            pltpu.VMEM((2, SPAN, width), BF16),
            pltpu.VMEM(many, BF16),
            pltpu.VMEM((2, D, HD), BF16),
            pltpu.SemaphoreType.DMA((30,)),
        ],
    )(
        bias, gains, *lses, *stay(arrays[:2]), *arrays[2:4], *stay(arrays[4:9]), *arrays[9:],
        *weights, *stay(sums[:2]), *sums[2:],
    )


def input_back_kernel(
    gain_ref, x_hbm, dya_hbm, dyb_hbm, dqa_hbm, dqb_hbm, dka_hbm, dva_hbm, dkb_hbm, dvb_hbm,
    halo_hbm, wkv_hbm, w0_hbm, w1_hbm, w2_hbm, w3_hbm, tg_hbm,
    x, dy, dq, own, old, halo, wkv, w, tg, sems,
):
    rows_all = x.shape[0]
    copies = Copies(sems)
    first = [
        copies.load(dka_hbm, own.at[0]),
        copies.load(dva_hbm, own.at[1]),
        copies.load(dkb_hbm, old.at[0]),
        copies.load(dvb_hbm, old.at[1]),
        copies.load(halo_hbm, halo),
        copies.load(wkv_hbm, wkv),
        copies.load(dqb_hbm, dq.at[pl.ds(0, WINDOW)]),
        copies.load(dqa_hbm, dq.at[pl.ds(WINDOW, WINDOW)]),
    ]
    first += [
        copies.load(p.at[0], w.at[i]) for i, p in enumerate((w0_hbm, w1_hbm, w2_hbm, w3_hbm))
    ]
    first.append(copies.load(x_hbm, x))
    first += [
        copies.load(dyb_hbm, dy.at[pl.ds(0, WINDOW)]),
        copies.load(dya_hbm, dy.at[pl.ds(WINDOW, WINDOW)]),
    ]
    for copy in first:
        copy.wait()
    gain = gain_ref[0:1, :]
    for block, rows in enumerate(blocks(rows_all)):
        grads = []
        for i in range(2):
            if block < 2:
                other = old[i, rows]
            else:
                other = halo[i, (block - 2) * BLOCK : (block - 1) * BLOCK].astype(F32)
            grads.append((own[i, rows] + other).astype(BF16))
        dh = dot_nt(grads[0], wkv[0]) + dot_nt(grads[1], wkv[1])
        for head in range(HEADS):
            dh = dh + dot_nt(dq[rows, head * HD : (head + 1) * HD], w[head])
        values = x[rows].astype(F32)
        r = lax.rsqrt(row_mean(values * values) + EPSILON)
        n = values * r
        inner = dh * gain
        tg[rows] = dy[rows] + r * (inner - n * row_mean(inner * n))
        copies.store(tg.at[rows], tg_hbm.at[rows])
    copies.finish()


def input_back(gains, arrays, weights):
    rows = arrays[0].shape[0]
    width = HEADS * HD
    return call(
        input_back_kernel,
        LONG,
        24,
        in_specs=[IN_VMEM] + [ANYWHERE] * 15,
        out_specs=ANYWHERE,
        out_shape=in_hbm((rows, D), F32),
        scratch_shapes=[
            pltpu.VMEM((rows, D), BF16),
            pltpu.VMEM((rows, D), F32),
            pltpu.VMEM((rows, width), BF16),
            pltpu.VMEM((2, rows, HD), F32),
            pltpu.VMEM((2, WINDOW, HD), F32),
            pltpu.VMEM((2, WINDOW, HD), BF16),
            pltpu.VMEM((2, D, HD), BF16),
            pltpu.VMEM((HEADS, D, HD), BF16),
            pltpu.VMEM((rows, D), F32),
            pltpu.SemaphoreType.DMA((24,)),
        ],
    )(gains, arrays[0], *stay(arrays[1:9]), *arrays[9:], *weights)


def ff_kernel(packed, first_call, last_call, h_hbm, ht_hbm, c_hbm, ct_hbm, *rest):
    if packed:
        w_hbm, rest = [rest[0].at[i] for i in range(3)], rest[1:]
    else:
        w_hbm, rest = rest[:3], rest[3:]
    if not first_call:
        m_in, d_in = rest[:2]
        rest = rest[2:]
    if last_call:
        y_hbm, rest = rest[0], rest[1:]
    g_hbm, m_hbm, d_hbm, h, ht, c, ct, w, g, m_sum, d_sum, f_all, dg_all, du_all = rest[:14]
    rest = rest[14:]
    copies = Copies(rest[-1])
    first = [copies.load(h_hbm, h)] + [copies.load(w_hbm[i], w.at[i]) for i in range(2)]
    first += [copies.load(c_hbm, c), copies.load(w_hbm[2], w.at[2])]
    second = []
    if not first_call:
        m_old, d_old = rest[:2]
        rest = rest[2:]
        second += [copies.load(m_in, m_old), copies.load(d_in, d_old)]
    if last_call:
        y, out = rest[:2]
        second.append(copies.load(y_hbm, y))
    third = [copies.load(ht_hbm, ht), copies.load(ct_hbm, ct)]
    for copy in first:
        copy.wait()
    for block, rows in enumerate(blocks(h.shape[0], 2 * BLOCK)):
        gate = dot(h[rows], w[0])
        up = dot(h[rows], w[1])
        df = dot(c[rows], w[2])
        square = gate * gate
        th = jnp.tanh(gate * (GELU_A + GELU_B * square))
        half = 0.5 + 0.5 * th
        gelu = gate * half
        slope = half + gelu * (1.0 - th) * (GELU_A + 3.0 * GELU_B * square)
        f = (gelu * up).astype(BF16)
        dg = (df * up * slope).astype(BF16)
        du = (df * gelu).astype(BF16)
        f_all[rows] = f
        dg_all[rows] = dg
        du_all[rows] = du
        m = dot_nt(f, w[2])
        d = dot_nt(dg, w[0]) + dot_nt(du, w[1])
        if block == 0:
            for copy in second:
                copy.wait()
        if not first_call:
            m = m + m_old[rows]
            d = d + d_old[rows]
        if last_call:
            out[rows] = (y[rows] + m).astype(BF16)
        else:
            m_sum[rows] = m
        d_sum[rows] = d
    copies.store(out if last_call else m_sum, m_hbm)
    copies.store(d_sum, d_hbm)
    for copy in third:
        copy.wait()
    g[0] = dot(ht[...], dg_all[...]).astype(BF16)
    g[1] = dot(ht[...], du_all[...]).astype(BF16)
    g[2] = dot(ct[...], f_all[...]).astype(BF16)
    copies.store(g, g_hbm)
    copies.finish()


def feed_forward(h, h_t, c, c_t, weights, sums=(), y=()):
    rows = h.shape[0]
    total = pltpu.VMEM((rows, D), F32)
    return call(
        functools.partial(ff_kernel, len(weights) == 1, not sums, bool(y)),
        LONG if sums else SHORT,
        44,
        in_specs=[ANYWHERE] * (4 + len(weights)) + [IN_HBM] * (len(sums) + len(y)),
        out_specs=[ANYWHERE, IN_HBM, IN_HBM],
        out_shape=[
            shape((3, D, PART), BF16),
            in_hbm((rows, D), BF16 if y else F32),
            in_hbm((rows, D), F32),
        ],
        scratch_shapes=[
            pltpu.VMEM((rows, D), BF16),
            pltpu.VMEM((D, rows), BF16),
            pltpu.VMEM((rows, D), BF16),
            pltpu.VMEM((D, rows), BF16),
            pltpu.VMEM((3, D, PART), BF16),
            pltpu.VMEM((3, D, PART), BF16),
            total,
            total,
        ]
        + [pltpu.VMEM((rows, PART), BF16)] * 3
        + [total] * len(sums)
        + ([total, pltpu.VMEM((rows, D), BF16)] if y else [])
        + [pltpu.SemaphoreType.DMA((14,))],
    )(h, h_t, c, c_t, *weights, *stay(sums), *stay(y))


def pack_small_kernel(kv_ref, gain_ref, x_hbm, out_ref, halo_ref, sems):
    copies = Copies(sems)
    load = copies.load(x_hbm.at[pl.ds(x_hbm.shape[0] - WINDOW, WINDOW)], halo_ref)
    out_ref[:KV_ROWS] = kv_ref[0].astype(BF16)
    out_ref[KV_ROWS : 2 * KV_ROWS] = kv_ref[1].astype(BF16)
    out_ref[2 * KV_ROWS :] = jnp.zeros((32, HD), BF16)
    out_ref[2 * KV_ROWS : 2 * KV_ROWS + 2, :KV_ROWS] = gain_ref[...].astype(BF16)
    load.wait()


def pack_small(key_value, gains, tokens):
    return call(
        pack_small_kernel,
        SHORT,
        12,
        in_specs=[IN_VMEM, IN_VMEM, ANYWHERE],
        out_specs=[IN_VMEM, IN_VMEM],
        out_shape=[shape((2 * KV_ROWS + 32, HD), BF16), shape((WINDOW, D), BF16)],
        scratch_shapes=[pltpu.SemaphoreType.DMA((1,))],
    )(key_value, gains, *stay([tokens]))


def pack_kernel(half_ref, q_hbm, o_hbm, gu_hbm, d_hbm, *rest):
    wide_hbm, half_hbm, hidden_hbm, gate_hbm, up_hbm, q, o, gu, d, wide, hidden, sems = rest
    copies = Copies(sems)
    loads = [copies.load(q_hbm, q), copies.load(o_hbm, o)]
    loads += [copies.load(d_hbm, d), copies.load(gu_hbm, gu)]
    loads[0].wait()
    wide[0] = q[...].astype(BF16)
    loads[1].wait()
    wide[1] = o[...].T.astype(BF16)
    copies.store(wide, wide_hbm)
    loads[2].wait()
    hidden[2] = d[...].T.astype(BF16)
    start = pl.multiple_of(half_ref[0] * (D // 2), D // 2)
    copies.store(hidden.at[2, pl.ds(start, D // 2)], half_hbm)
    loads[3].wait()
    hidden[:2] = gu[...].astype(BF16)
    copies.store(hidden.at[0], gate_hbm)
    copies.store(hidden.at[1], up_hbm)
    copies.store(hidden, hidden_hbm)
    copies.finish()


def pack(half, query, output, gate_up, down):
    matrix = shape((D, PART), BF16)
    wide, hidden = shape((2, D, HD), BF16), shape((3, D, PART), BF16)
    return call(
        pack_kernel,
        LONG,
        14,
        in_specs=[IN_SMEM] + [ANYWHERE] * 4,
        out_specs=[ANYWHERE] * 5,
        out_shape=[wide, shape((D // 2, PART), BF16), hidden, matrix, matrix],
        scratch_shapes=[
            pltpu.VMEM(v.shape, F32) for v in (query, output, gate_up, down)
        ]
        + [pltpu.VMEM(o.shape, BF16) for o in (wide, hidden)]
        + [pltpu.SemaphoreType.DMA((10,))],
    )(half, *stay([query, output, gate_up, down]))


def adam_step(weight, first, second, grad, rate):
    first_new = BETA_ONE * first + (1.0 - BETA_ONE) * grad
    second_new = BETA_TWO * second + (1.0 - BETA_TWO) * grad * grad
    first_hat = first_new / (1.0 - BETA_ONE**STEP)
    second_hat = second_new / (1.0 - BETA_TWO**STEP)
    updated = weight - rate * (
        first_hat / (jnp.sqrt(second_hat) + ADAM_EPSILON) + WEIGHT_DECAY * weight
    )
    return (updated, first_new, second_new)


def adam_flip_kernel(rate, w_ref, m_ref, v_ref, g_ref, w_out, m_out, v_out):
    w_out[...], m_out[...], v_out[...] = adam_step(
        w_ref[...], m_ref[...], v_ref[...], g_ref[...].astype(F32).T, rate
    )


def adam_flip(weight, first, second, grad, rate):
    state = pl.BlockSpec((128, D), lambda i: (i, 0))
    return call(
        functools.partial(adam_flip_kernel, rate),
        3 << 30,
        16,
        grid=(weight.shape[0] // 128,),
        in_specs=[state] * 3 + [pl.BlockSpec((D, 128), lambda i: (0, i))],
        out_specs=[state] * 3,
        out_shape=[shape(weight.shape, F32)] * 3,
    )(weight, first, second, grad)


def adam_plane_kernel(rate, w_ref, m_ref, v_ref, g_ref, *rest):
    w_out, m_out, v_out = rest[-3:]
    grad = g_ref[...].astype(F32)
    w_out[0], m_out[0], v_out[0] = adam_step(w_ref[0], m_ref[0], v_ref[0], grad, rate)


def adam_plane(plane, weight, first, second, grad, rate, partial=()):
    rows = D // 4
    state = pl.BlockSpec((1, rows, PART), lambda i: (plane, i, 0))
    return call(
        functools.partial(adam_plane_kernel, rate),
        4 << 30,
        24,
        grid=(4,),
        in_specs=[state] * 3
        + [pl.BlockSpec((rows, PART), lambda i: (i, 0))]
        + [ANYWHERE] * len(partial),
        out_specs=[state] * 3,
        out_shape=[shape(weight.shape, F32)] * 3,
        input_output_aliases={4: 0, 5: 1, 6: 2} if partial else {},
    )(weight, first, second, grad, *partial)


def swap(value, axis, mask):
    count = lax.axis_size(axis)
    return lax.ppermute(value, axis, [(i, i ^ mask) for i in range(count)])


def shifted(value, axis, steps):
    count = lax.axis_size(axis)
    leading, last = (max(0, -steps), min(count, count - steps))
    return lax.ppermute(value, axis, [(source, source + steps) for source in range(leading, last)])


def after(value, *others):
    return lax.optimization_barrier((value, *others))[0]


def by_index(parts, index):
    core, side = (index & 1) == 1, (index & 2) == 2
    a = jnp.where(core, parts[1], parts[0])
    b = jnp.where(core, parts[0], parts[1])
    c = jnp.where(core, parts[3], parts[2])
    d = jnp.where(core, parts[2], parts[3])
    return [
        jnp.where(side, c, a),
        jnp.where(side, d, b),
        jnp.where(side, a, c),
        jnp.where(side, b, d),
    ]


def add(*values):
    return functools.reduce(lambda a, b: a + b, [v.astype(F32) for v in values]).astype(BF16)


def replica_levels():
    bits = lax.axis_size("dp").bit_length() - 1
    levels = [[1]]
    for low in range(1, bits, 2):
        levels.append([m << low for m in ((1, 2, 3) if low + 1 < bits else (1,))])
    return levels


def place(level):
    return (lax.axis_index("dp") // level[0]) % (len(level) + 1)


def by_place(parts, level):
    if len(level) == 3:
        return by_index(parts, place(level))
    high = place(level) == 1
    return [jnp.where(high, parts[1], parts[0]), jnp.where(high, parts[0], parts[1])]


def rows_by_place(value):
    sizes = [len(level) + 1 for level in reversed(replica_levels())]
    rows = value.shape[-2] // lax.axis_size("dp")
    return value.reshape(*value.shape[:-2], *sizes, rows, value.shape[-1])


def rows_joined(value, dims):
    return value.reshape(*value.shape[:dims], -1, value.shape[-1])


def cut(value, level):
    count = len(level) + 1
    return by_place([value[..., i, :, :] for i in range(count)], level)


def send(shares, level):
    return [swap(share, "dp", mask) for share, mask in zip(shares, level)]


def fill(shares, level):
    parts = by_place(shares, level)
    whole_rows = jnp.concatenate(parts, axis=-2)
    lead, last = whole_rows.shape[:-2], whole_rows.shape[-1]
    return whole_rows.reshape(*lead, len(parts), -1, last)


def half_sum(shares):
    return jnp.stack(shares[1:3])


def reduce_over(value, levels):
    for level in levels:
        shares = cut(value, level)
        value = add(shares[0], *send(shares[1:], level))
    return value


def gather_over(value, levels):
    for level in reversed(levels):
        value = fill([value] + send([value] * len(level), level), level)
    return value


def sum_over(value, levels):
    for level in levels:
        for mask in level[:: max(len(level) - 1, 1)]:
            value = add(value, swap(value, "dp", mask))
    return value


def hold(values, *others):
    return lax.optimization_barrier((tuple(values), others))[0]


def small_chunks(wkv_grad, gain_grads, shard):
    chunks = []
    for t in range(4):
        rows = slice(t * KV_ROWS, (t + 1) * KV_ROWS)
        gains = jnp.pad(gain_grads[:, rows].astype(BF16), ((0, 30), (0, HD - KV_ROWS)))
        chunks.append(
            jnp.concatenate([wkv_grad[:, rows].reshape(2 * KV_ROWS, HD), gains], axis=0)
        )
    chunks = by_index(chunks, shard)
    return jnp.stack(chunks[1::2]), chunks[::2]


def rate_list():
    return (
        2.0 / D**0.5,
        2.0 / D**0.5,
        2.0 / (HEADS * HD // (WINDOW // 2)) ** 0.5,
        2.0 / D**0.5,
        2.0 / FF**0.5,
        GAIN_RATE,
    )


def per_device(
    tokens,
    out_grad,
    query_weight,
    query_first,
    query_second,
    key_value_weight,
    key_value_first,
    key_value_second,
    output_weight,
    output_first,
    output_second,
    gate_up_weight,
    gate_up_first,
    gate_up_second,
    down_weight,
    down_first,
    down_second,
    gain_values,
    gain_first,
    gain_second,
):
    shard = lax.axis_index("shard")
    rows = tokens.shape[0]
    levels = replica_levels()
    pair, rest = levels[0], levels[1:]
    quad = rest[0]

    small, last_tokens = pack_small(key_value_weight, gain_values, tokens)
    small_side = swap(small, "shard", 2)
    small_core = swap(small, "shard", 1)
    halo = shifted(last_tokens, "shard", 1)
    early = lax.optimization_barrier(
        (query_weight, output_weight, gate_up_weight, down_weight, small_side)
    )[:4]
    half = place(pair).astype(jnp.int32).reshape(1)
    wide, down_half, hidden, gate, up = pack(half, *early)
    halo, small_diagonal = hold(
        [halo, swap(small_side, "shard", 1)], wide
    )
    wide_side = swap(wide, "shard", 2)
    wide_core = swap(wide, "shard", 1)
    down_half = swap(down_half, "shard", 2)
    gate_side = swap(gate, "shard", 2)
    up_side = swap(up, "shard", 2)
    hidden_core = swap(hidden, "shard", 1)
    out_grad_t = out_grad.T

    ordered = by_index([small, small_core, small_side, small_diagonal], shard)
    wkv = jnp.concatenate([o[: 2 * KV_ROWS].reshape(2, KV_ROWS, HD) for o in ordered], axis=1)
    gains = jnp.concatenate(
        [o[2 * KV_ROWS : 2 * KV_ROWS + 2, :KV_ROWS] for o in ordered], axis=1
    ).astype(F32)
    gains = after(gains, wide, out_grad_t)

    normed, normed_t, kv = key_value(halo, tokens, gains, wkv)
    bias = jnp.where(shard == 0, NEGATIVE, 0.0).astype(F32).reshape(1)
    q_near, a_near, lse_near, y_near = attend(
        bias, gains, normed, kv, (wide, wide_core), tokens, False
    )
    wide_side = after(wide_side, lse_near)
    hidden_core = after(hidden_core, lse_near)
    wide_diagonal = swap(wide_side, "shard", 1)
    q_far, a_far, lse_far, middle, second_norm, second_norm_t = attend(
        bias, gains, normed, kv, (wide_side, wide_diagonal), y_near, True
    )

    ff = lambda h, *more: feed_forward(h, second_norm_t, out_grad, out_grad_t, *more)
    g1, *sums = ff(second_norm, (hidden_core,))
    gate_side, down_half = hold([gate_side, down_half], g1)
    down_other = swap(down_half, "dp", pair[0])
    g0, *sums = ff(after(second_norm, gate_side, down_half), (hidden,), sums)
    g1 = after(swap(g1, "shard", 1), g0)
    near_shares = cut(rows_by_place(add(g0[:2], g1[:2])), pair)
    near_third = add(g0[2], g1[2])
    up_side = after(up_side, g0)
    gate_diagonal = swap(gate_side, "shard", 1)
    up_diagonal = swap(up_side, "shard", 1)
    down_side = rows_joined(fill([down_half, after(down_other, g0)], pair), 0)
    down_diagonal = swap(down_side, "shard", 1)
    g2, *sums = ff(
        after(second_norm, near_shares[1]), (gate_side, up_side, down_side), sums
    )
    diagonal = (gate_diagonal, up_diagonal, down_diagonal)
    g3, block_output, d_sum = ff(second_norm, diagonal, sums, (middle,))
    g2 = after(swap(g2, "shard", 1), g3)
    near_two = add(near_shares[0], after(send(near_shares[1:], pair)[0], g3))
    near_cut = cut(near_two, quad)
    far_shares = cut(rows_by_place(add(g3[:2], g2[:2])), pair)
    far_third = add(g3[2], g2[2])

    wides = (wide, wide_core, wide_side, wide_diagonal)
    arrays = (middle, out_grad, kv, q_near, q_far, a_near, a_far, normed_t, wkv)
    d_sum = after(d_sum, far_third, far_shares[1], near_cut[1])
    dy_b, dq_b, dk_b, dv_b, *sums, halo_out = attend_back(
        0, bias, gains, (lse_near, lse_far), (d_sum, *arrays), wides, ()
    )
    halo_grad = shifted(halo_out, "shard", -1)
    pin = sums[2]
    near_done = add(near_cut[0], *[after(v, pin) for v in send(near_cut[1:], quad)])
    far_two = add(far_shares[0], after(send(far_shares[1:], pair)[0], pin))
    far_cut = cut(far_two, quad)
    third = add(near_third, after(swap(far_third, "shard", 3), pin))
    third_shares = cut(rows_by_place(third), pair)
    d_sum = after(d_sum, far_cut[1], third_shares[1], near_done)
    dy_a, dq_a, dk_a, dv_a, wide_even, wide_odd, wkv_grad, gain_grads = attend_back(
        1, bias, gains, (lse_near, lse_far), (d_sum, *arrays), wides, sums
    )


    more = rest[1:]
    near_mask, far_mask = quad[0], quad[-1]
    dp_swap = lambda value, mask: swap(value, "dp", mask)
    arrived = hold(
        [halo_grad, *send(third_shares[1:], pair), *send(far_cut[1:], quad)], gain_grads
    )
    halo_grad = arrived[0]
    wide_odd, wkv_grad, third_own, far_own = hold(
        [wide_odd, wkv_grad, third_shares[0], far_cut[0]], *arrived
    )
    third = add(third_own, arrived[1])
    far_done = add(far_own, *arrived[2:])
    small_pair, small_even = small_chunks(wkv_grad, gain_grads, shard)
    far_done, near_done = reduce_over(far_done, more), reduce_over(near_done, more)
    shares = cut(third, quad)
    third_sent = jnp.stack(shares[1:3])
    got_wide = hold([swap(wide_odd, "shard", 1)], small_pair, far_done, third_sent)[0]
    wide_far = add(wide_even[1], got_wide[1])
    wide_near = add(wide_even[0], got_wide[0])
    dk_a = after(dk_a, wide_far)
    tokens_grad = input_back(
        gains,
        (tokens, dy_a, dy_b, dq_a, dq_b, dk_a, dv_a, dk_b, dv_b, halo_grad, wkv),
        wides,
    )
    got_small, got_two, got_third = hold(
        [
            swap(small_pair, "shard", 1),
            swap(far_done, "shard", 3),
            dp_swap(third_sent, near_mask),
        ],
        tokens_grad,
    )
    small_far = add(small_even[1], got_small[1])
    small_near = add(small_even[0], got_small[0])
    two = gather_over(add(near_done, got_two), more)
    third_mine, third_sent = add(shares[0], got_third[0]), add(shares[3], got_third[1])
    got_wide = hold([swap(wide_far, "shard", 2)], small_far, two, third_sent)[0]
    wide_shares = cut(rows_by_place(add(wide_near, got_wide)), pair)
    two_far = hold([dp_swap(two, far_mask)], wide_shares[1])[0]
    two_pair = jnp.stack([two, two_far])
    got_small, got_third = hold(
        [swap(small_far, "shard", 2), dp_swap(third_sent, far_mask)], two_pair
    )
    small_shares = cut(rows_by_place(add(small_near, got_small)), pair)
    third = add(third_mine, got_third)
    third = gather_over(reduce_over(third, more), more)
    near_pair = lambda shares: jnp.stack(shares[1:3])
    got_wide = hold(
        [dp_swap(wide_shares[1], pair[0])], small_shares[1], two_pair, third
    )[0]
    wide_cut = cut(add(wide_shares[0], got_wide), quad)
    wide_sent = near_pair(wide_cut)
    got_small, third_far = hold(
        [dp_swap(small_shares[1], pair[0]), dp_swap(third, far_mask)], wide_sent
    )
    small_sum = add(small_shares[0], got_small)
    third_pair = jnp.stack([third, third_far])
    got_wide, got_two = hold(
        [dp_swap(wide_sent, near_mask), dp_swap(two_pair, near_mask)], small_sum, third_pair
    )
    wide_mine, wide_sent = add(wide_cut[0], got_wide[0]), add(wide_cut[3], got_wide[1])
    two = fill([two, got_two[0], got_two[1], two_far], quad)
    got_small, got_third = hold(
        [dp_swap(small_sum, near_mask), dp_swap(third_pair, near_mask)], wide_sent, two
    )
    small_sum = add(small_sum, got_small)
    third = fill([third, got_third[0], got_third[1], third_far], quad)
    got_wide = hold([dp_swap(wide_sent, far_mask)], small_sum, third)[0]
    wide_sum = add(wide_mine, got_wide)
    wide_sum = gather_over(reduce_over(wide_sum, more), more)
    got_small, gate_x = hold(
        [dp_swap(small_sum, far_mask), dp_swap(two[0], pair[0])], wide_sum
    )
    small_sum = sum_over(add(small_sum, got_small), more)
    rates = rate_list()
    joined = lambda mine, other, dims: rows_joined(fill([mine, other], pair), dims)
    wide_far = hold([dp_swap(wide_sum, far_mask)], small_sum, gate_x)[0]
    wide_pair = jnp.stack([wide_sum, wide_far])
    gate_update = adam_plane(
        0,
        gate_up_weight,
        gate_up_first,
        gate_up_second,
        joined(two[0], after(gate_x, wide_pair), 0),
        rates[3],
    )
    up_x = hold([dp_swap(two[1], pair[0])], gate_update[0])[0]
    gate_up_update = adam_plane(
        1,
        gate_up_weight,
        gate_up_first,
        gate_up_second,
        joined(two[1], up_x, 0),
        rates[3],
        gate_update,
    )
    got_wide, got_small = hold(
        [dp_swap(wide_pair, near_mask), dp_swap(small_sum, pair[0])], gate_up_update[0]
    )
    wide_sum = fill([wide_sum, got_wide[0], got_wide[1], wide_far], quad)
    small_grad = joined(small_sum, after(got_small, wide_sum), 0)
    key_value_update = adam_step(
        key_value_weight,
        key_value_first,
        key_value_second,
        small_grad[: 2 * KV_ROWS].reshape(2, KV_ROWS, HD).astype(F32),
        rates[1],
    )
    gain_update = adam_step(
        gain_values,
        gain_first,
        gain_second,
        small_grad[2 * KV_ROWS : 2 * KV_ROWS + 2, :KV_ROWS].astype(F32),
        rates[5],
    )
    third_x = hold([dp_swap(third, pair[0])], wide_sum)[0]
    down_update = adam_flip(
        down_weight, down_first, down_second, joined(third, third_x, 0), rates[4]
    )
    got_wide = hold(
        [dp_swap(wide_sum, pair[0])], down_update[0], key_value_update[0], gain_update[0]
    )[0]
    wide_grad = joined(wide_sum, got_wide, 1)
    query_update = adam_step(
        query_weight, query_first, query_second, wide_grad[0].astype(F32), rates[0]
    )
    output_update = adam_flip(output_weight, output_first, output_second, wide_grad[1], rates[2])
    return (
        block_output,
        tokens_grad,
        *query_update,
        *key_value_update,
        *output_update,
        *gate_up_update,
        *down_update,
        *gain_update,
    )


def solution(mesh):
    token_spec = P(("dp", "shard"), None)
    state_specs = (
        (P(None, "shard"),) * 3
        + (P(None, "shard", None),) * 3
        + (P("shard", None),) * 3
        + (P(None, None, "shard"),) * 3
        + (P("shard", None),) * 3
        + (P(None, "shard"),) * 3
    )
    specs = (token_spec, token_spec) + state_specs
    return jax.shard_map(
        per_device, mesh=mesh, in_specs=specs, out_specs=specs, check_vma=False
    )
```
